32 devices in a mesh: groups: 2 (over x), seq: 16 (over z, y, core).
Axes of the slice: x: 2, y: 2, z: 4, core: 2. Of those that a mesh axis runs over, the one named last changes fastest.
Arguments:
- queries: bfloat16 [8192, 2048], P(('groups', 'seq')), parts along dimension 0, may hold values from -9 to 9
- keys_in: bfloat16 [8192, 2048], P(('groups', 'seq')), parts along dimension 0, may hold values from -9 to 9
- values_in: bfloat16 [8192, 2048], P(('groups', 'seq')), parts along dimension 0, may hold values from -6 to 6
- cotangent: bfloat16 [8192, 2048], P(('groups', 'seq')), parts along dimension 0, may hold values from -6 to 6
- matching: int32 [32], P('groups'), parts along dimension 0, may hold values from 0 to 15, each once
- assign: int32 [32, 16], P('groups'), parts along dimension 0, may hold values from 0 to 15
Outputs:
- attended: bfloat16 [8192, 2048], P(('groups', 'seq')), parts along dimension 0
- grad_queries: bfloat16 [8192, 2048], P(('groups', 'seq')), parts along dimension 0
- grad_keys: bfloat16 [8192, 2048], P(('groups', 'seq')), parts along dimension 0
- grad_values: bfloat16 [8192, 2048], P(('groups', 'seq')), parts along dimension 0
The draws below stay inside these ranges and needn't reach their ends.
There are 2 independent parts, one for each index of `groups`. The reference program is written for one: setup_inputs(seed, part) draws one part's arguments, and reference() takes and returns one part's arrays. A program takes and returns all parts, laid end to end along the dimension named above; each array names one. Nothing has to cross between parts.
Inputs may be any that keep to these rules, and one draw needn't show every extreme that they name: `matching`: each block index appears once.
All inputs are finite; a program needn't handle non-finite values.
Results may differ from the reference program's by a relative error of at most 0.019.
Values may be sent and summed in bfloat16 or wider, within the bound.
A program may use at most 128 MiB of HBM per device.

```python
import math
import jax
import jax.numpy as jnp
import numpy as np
from jax import lax

BLOCK = 256
HEADS = 16
HEAD_DIM = 128
NB = 16
SEQ = 4096
WIDTH = 2048


def base_pair(key):
    first_key, second = jax.random.split(jax.random.fold_in(key, 17))
    queries = jnp.clip(jax.random.normal(first_key, (SEQ, WIDTH), jnp.float32), -4.0, 4.0)
    keys_base = jnp.clip(jax.random.normal(second, (SEQ, WIDTH), jnp.float32), -4.0, 4.0)
    return (queries, keys_base)


def drawn(key):
    queries, keys_base = base_pair(key)
    return (queries, keys_base)


def draw_queries(key, part):
    return drawn(key)[0].astype(jnp.bfloat16)


def draw_keys_in(key, part):
    return drawn(key)[1].astype(jnp.bfloat16)


def plant(drawn, own_key, least, high):
    dims = drawn.shape
    index_at = [jax.random.randint(jax.random.fold_in(own_key, axis), (), 0, dims[axis]) for axis in range(len(dims))]
    drawn = drawn.at[tuple(index_at)].set(least)
    longest = dims.index(max(dims))
    index_at[longest] = (index_at[longest] + 1) % dims[longest]
    return drawn.at[tuple(index_at)].set(high)


def levels(own_key, shape, cuts, low, largest):
    factor_of = 1.0
    for position, shards_of in cuts:
        heights = jax.random.uniform(jax.random.fold_in(jax.random.fold_in(own_key, 6), position), (shards_of,), jnp.float32, low / len(cuts), largest / len(cuts))
        factor_of = factor_of * jnp.repeat(jnp.exp(heights), shape[position] // shards_of).reshape((-1,) + (1,) * (len(shape) - 1 - position))
    return factor_of


def cumulative_ranks(number_of, slope):
    loads = [(1 << 20) // math.isqrt(grade ** slope) + 1 for grade in range(1, number_of + 1)]
    spread = 1 + sum(loads) // (1 << 30)
    return np.cumsum(np.array([max(1, weight // spread) for weight in loads]))


def ranked(stream_key, shape, amount, skew):
    listing = cumulative_ranks(amount, skew)
    pick = jax.random.randint(jax.random.fold_in(stream_key, 1), shape, 0, int(listing[amount - 1]))
    grade = jnp.searchsorted(jnp.asarray(listing, jnp.int32), pick, side="right")
    return jax.random.permutation(jax.random.fold_in(stream_key, 2), amount)[grade].astype(jnp.int32)


def normal_values(key, extent, width, limit, cuts=(), held_as=jnp.bfloat16):
    factor_of = levels(key, extent, cuts, -0.22, 0.18) if cuts else 1.0
    drawn = jax.random.normal(key, extent, jnp.float32) * width * factor_of
    return jnp.minimum(jnp.maximum(drawn, -limit), limit).astype(held_as)


def setup_inputs(seed: int = 0, part: int = 0) -> dict:
    seeds = jax.random.split(jax.random.key(seed), 7)
    own_keys = jax.random.split(jax.random.fold_in(seeds[6], part), 7)
    return {
        "queries": draw_queries(jax.random.fold_in(jax.random.fold_in(seeds[6], part), 71), part),
        "keys_in": draw_keys_in(jax.random.fold_in(jax.random.fold_in(seeds[6], part), 71), part),
        "values_in": normal_values(own_keys[2], (SEQ, WIDTH), 1.0, 6.0, ((0, 16),)),
        "cotangent": normal_values(own_keys[3], (SEQ, WIDTH), 1.0, 6.0, ((0, 16),)),
        "matching": jax.random.permutation(own_keys[4], NB).astype(jnp.int32),
        "assign": plant(ranked(own_keys[5], (HEADS, NB), NB, 2), jax.random.fold_in(own_keys[5], 3), 0, NB - 1).astype(jnp.int32),
    }


def one_block(block, query_all, keys_all, values_all, cot_all, partner):
    heads_at = jnp.arange(HEADS, dtype=jnp.int32)
    chosen = partner[:, block]
    factor = HEAD_DIM ** -0.5
    query_here = query_all[block].astype(jnp.float32)
    cot_here = cot_all[block].astype(jnp.float32)
    far_key = keys_all[chosen, :, heads_at, :].transpose(1, 0, 2)
    far_value = values_all[chosen, :, heads_at, :].transpose(1, 0, 2)
    key_cat = jnp.concatenate([keys_all[block], far_key], axis=0).astype(jnp.float32)
    value_cat = jnp.concatenate([values_all[block], far_value], axis=0).astype(jnp.float32)
    scores = jnp.einsum('qhd,khd->hqk', query_here, key_cat) * factor
    highest = jnp.max(scores, axis=-1, keepdims=True)
    raised = jnp.exp(scores - highest)
    weights = raised / jnp.sum(raised, axis=-1, keepdims=True)
    weights_low = weights.astype(jnp.bfloat16).astype(jnp.float32)
    attended = jnp.einsum('hqk,khd->qhd', weights_low, value_cat).astype(jnp.bfloat16)
    dprobs = jnp.einsum('qhd,khd->hqk', cot_here, value_cat)
    row_dot = jnp.einsum('qhd,qhd->hq', cot_here, attended.astype(jnp.float32))
    dscores = (weights * (dprobs - row_dot[..., None]) * factor).astype(jnp.bfloat16).astype(jnp.float32)
    grad_query = jnp.einsum('hqk,khd->qhd', dscores, key_cat).astype(jnp.bfloat16)
    dkey_cat = jnp.einsum('hqk,qhd->khd', dscores, query_here)
    dvalue_cat = jnp.einsum('hqk,qhd->khd', weights_low, cot_here)
    return (attended, grad_query, dkey_cat[:BLOCK], dvalue_cat[:BLOCK],
            dkey_cat[BLOCK:].astype(jnp.bfloat16), dvalue_cat[BLOCK:].astype(jnp.bfloat16))


def partner_sum(far_terms, partner):
    def head_sum(head):
        column = lax.dynamic_index_in_dim(far_terms, head, 2, keepdims=False).astype(jnp.float32)
        return jax.ops.segment_sum(column, partner[head], num_segments=NB)
    summed = lax.map(head_sum, jnp.arange(HEADS, dtype=jnp.int32))
    return summed.transpose(1, 2, 0, 3).astype(jnp.bfloat16)


def reference(queries, keys_in, values_in, cotangent, matching, assign):
    partner = jnp.take(matching, assign, axis=0).astype(jnp.int32)
    shape4 = (NB, BLOCK, HEADS, HEAD_DIM)
    query_all = queries.reshape(shape4)
    keys_all = keys_in.reshape(shape4)
    values_all = values_in.reshape(shape4)
    cot_all = cotangent.reshape(shape4)
    results = lax.map(lambda block: one_block(block, query_all, keys_all, values_all, cot_all, partner),
                      jnp.arange(NB, dtype=jnp.int32))
    attended, grad_query, dkey_own, dvalue_own, far_keys, far_values = results
    recv_keys = partner_sum(far_keys, partner)
    recv_values = partner_sum(far_values, partner)
    grad_keys = (dkey_own + recv_keys.astype(jnp.float32)).astype(jnp.bfloat16)
    grad_values = (dvalue_own + recv_values.astype(jnp.float32)).astype(jnp.bfloat16)
    flat = (SEQ, WIDTH)
    return (attended.reshape(flat), grad_query.reshape(flat), grad_keys.reshape(flat), grad_values.reshape(flat))
```

```python
import functools

import jax
import jax.numpy as jnp
from jax import lax
from jax.experimental import pallas as pl
from jax.experimental.pallas import tpu as pltpu
from jax.sharding import PartitionSpec as P

BLOCK = 256
HEADS = 16
HEAD_DIM = 128


def to_columns(panel, seq_size, slice_width):
    blocks_dev = panel.shape[0] // BLOCK
    shaped = panel.reshape(blocks_dev, BLOCK, seq_size, slice_width).transpose(2, 0, 1, 3)
    return shaped.reshape(seq_size, blocks_dev, BLOCK * slice_width)


def from_columns(moved, seq_size, slice_width):
    blocks_dev = moved.shape[1]
    shaped = moved.reshape(seq_size, blocks_dev, BLOCK, slice_width).transpose(1, 2, 0, 3)
    return shaped.reshape(blocks_dev * BLOCK, seq_size * slice_width)


def by_columns(queries, keys_in, values_in, cotangent, matching, assign):
    seq_size = lax.axis_size("seq")
    tok_dev, feature_count = queries.shape
    blocks_dev = tok_dev // BLOCK
    total_blocks = matching.shape[0]
    partner = jnp.take(matching, assign, axis=0)
    targets = jnp.arange(total_blocks, dtype=jnp.int32)
    slice_width = feature_count // seq_size
    factor = HEAD_DIM ** (-0.5)

    def column_row():
        head_here = lax.axis_index("seq") * slice_width // HEAD_DIM
        return lax.dynamic_index_in_dim(partner, head_here, 0, keepdims=False)

    shape4 = (blocks_dev, BLOCK, HEADS, HEAD_DIM)
    query_blocks = queries.reshape(shape4)
    cot_blocks = cotangent.reshape(shape4)
    row_here = column_row()
    select_here = (targets[None, :] == row_here[:, None]).astype(jnp.bfloat16)

    def pick_one(piece):
        moved = jnp.dot(
            select_here, piece.reshape(total_blocks, -1), preferred_element_type=jnp.float32
        )
        return moved.astype(jnp.bfloat16).reshape(piece.shape)

    pieces = (
        lax.all_to_all(
            to_columns(keys_in, seq_size, slice_width),
            "seq",
            split_axis=0,
            concat_axis=0,
            tiled=True,
        ),
        lax.all_to_all(
            to_columns(values_in, seq_size, slice_width),
            "seq",
            split_axis=0,
            concat_axis=0,
            tiled=True,
        ),
    )
    got_first = lax.all_to_all(pick_one(pieces[0]), "seq", split_axis=0, concat_axis=0, tiled=True)
    got_second = lax.all_to_all(pick_one(pieces[1]), "seq", split_axis=0, concat_axis=0, tiled=True)
    key_far = from_columns(got_first, seq_size, slice_width)
    value_far = from_columns(got_second, seq_size, slice_width)
    key_cat = jnp.concatenate([keys_in.reshape(shape4), key_far.reshape(shape4)], axis=1)
    value_cat = jnp.concatenate([values_in.reshape(shape4), value_far.reshape(shape4)], axis=1)
    scores = (
        jnp.einsum("bqhd,bkhd->bhqk", query_blocks, key_cat, preferred_element_type=jnp.float32)
        * factor
    )
    highest = jnp.max(scores, axis=-1, keepdims=True)
    raised = jnp.exp(scores - highest)
    weights = raised / jnp.sum(raised, axis=-1, keepdims=True)
    key_cat, value_cat, weights, weights_low = (
        key_cat,
        value_cat,
        weights,
        weights.astype(jnp.bfloat16),
    )
    out_blocks = jnp.einsum(
        "bhqk,bkhd->bqhd", weights_low, value_cat, preferred_element_type=jnp.float32
    ).astype(jnp.bfloat16)
    dprobs = jnp.einsum(
        "bqhd,bkhd->bhqk", cot_blocks, value_cat, preferred_element_type=jnp.float32
    )
    row_dot = jnp.einsum(
        "bqhd,bqhd->bhq", cot_blocks, out_blocks, preferred_element_type=jnp.float32
    )
    dscores = (weights * (dprobs - row_dot[..., None]) * factor).astype(jnp.bfloat16)
    grad_query = jnp.einsum(
        "bhqk,bkhd->bqhd", dscores, key_cat, preferred_element_type=jnp.float32
    ).astype(jnp.bfloat16)
    dkey_cat = jnp.einsum(
        "bhqk,bqhd->bkhd", dscores, query_blocks, preferred_element_type=jnp.float32
    )
    dvalue_cat = jnp.einsum(
        "bhqk,bqhd->bkhd", weights_low, cot_blocks, preferred_element_type=jnp.float32
    )
    far_keys = dkey_cat[:, BLOCK:].astype(jnp.bfloat16).reshape(tok_dev, feature_count)
    far_values = dvalue_cat[:, BLOCK:].astype(jnp.bfloat16).reshape(tok_dev, feature_count)
    row_here = column_row()
    onehot_here = (row_here[None, :] == targets[:, None]).astype(jnp.bfloat16)

    def add_columns(piece):
        summed = jnp.dot(
            onehot_here, piece.reshape(total_blocks, -1), preferred_element_type=jnp.float32
        )
        return summed.astype(jnp.bfloat16).reshape(piece.shape)

    pieces = (
        lax.all_to_all(
            to_columns(far_keys, seq_size, slice_width),
            "seq",
            split_axis=0,
            concat_axis=0,
            tiled=True,
        ),
        lax.all_to_all(
            to_columns(far_values, seq_size, slice_width),
            "seq",
            split_axis=0,
            concat_axis=0,
            tiled=True,
        ),
    )
    got_first = lax.all_to_all(
        add_columns(pieces[0]), "seq", split_axis=0, concat_axis=0, tiled=True
    )
    got_second = lax.all_to_all(
        add_columns(pieces[1]), "seq", split_axis=0, concat_axis=0, tiled=True
    )
    recv_keys = from_columns(got_first, seq_size, slice_width)
    recv_values = from_columns(got_second, seq_size, slice_width)
    grad_keys = (
        dkey_cat[:, :BLOCK].reshape(tok_dev, feature_count) + recv_keys.astype(jnp.float32)
    ).astype(jnp.bfloat16)
    grad_values = (
        dvalue_cat[:, :BLOCK].reshape(tok_dev, feature_count) + recv_values.astype(jnp.float32)
    ).astype(jnp.bfloat16)
    return (
        out_blocks.reshape(tok_dev, feature_count),
        grad_query.reshape(tok_dev, feature_count),
        grad_keys,
        grad_values,
    )


def nt(a, b):
    return lax.dot_general(a, b, (((1,), (1,)), ((), ())), preferred_element_type=jnp.float32)


def tn(a, b):
    return lax.dot_general(a, b, (((0,), (0,)), ((), ())), preferred_element_type=jnp.float32)


def nn(a, b):
    return lax.dot_general(a, b, (((1,), (0,)), ((), ())), preferred_element_type=jnp.float32)


def head_kernel(
    n,
    matching,
    assign,
    q_ref,
    k_ref,
    v_ref,
    c_ref,
    att_ref,
    gq_ref,
    gk_ref,
    gv_ref,
    q_all,
    k_all,
    v_all,
    c_all,
    att_out,
    gq_out,
    gk_out,
    gv_out,
    own_k,
    own_v,
    sum_k,
    sum_v,
    part,
    in_send,
    in_recv,
    in_local,
    out_send,
    out_recv,
    out_local,
):
    me = lax.axis_index("seq")
    factor = HEAD_DIM ** (-0.5)
    power = factor * 1.4426950408889634
    ins = ((k_ref, k_all), (v_ref, v_all), (q_ref, q_all), (c_ref, c_all))
    outs = ((att_out, att_ref), (gq_out, gq_ref), (gk_out, gk_ref), (gv_out, gv_ref))

    def columns(index):
        return pl.ds(pl.multiple_of(index * HEAD_DIM, HEAD_DIM), HEAD_DIM)

    def scatter(a, to):
        src, dst = ins[a]
        return pltpu.make_async_remote_copy(
            src_ref=src.at[:, columns(to)],
            dst_ref=dst.at[me],
            send_sem=in_send.at[a, to],
            recv_sem=in_recv.at[a, me],
            device_id={"seq": to},
            device_id_type=pl.DeviceIdType.MESH,
        )

    def arrival(a, frm):
        src, dst = ins[a]
        return pltpu.make_async_remote_copy(
            src_ref=src.at[:, columns(frm)],
            dst_ref=dst.at[frm],
            send_sem=in_send.at[a, frm],
            recv_sem=in_recv.at[a, frm],
            device_id={"seq": frm},
            device_id_type=pl.DeviceIdType.MESH,
        )

    def stay(a):
        src, dst = ins[a]
        return pltpu.make_async_copy(src.at[:, columns(me)], dst.at[me], in_local.at[a])

    def give(a, to):
        src, dst = outs[a]
        return pltpu.make_async_remote_copy(
            src_ref=src.at[to],
            dst_ref=dst.at[:, columns(me)],
            send_sem=out_send.at[a, to],
            recv_sem=out_recv.at[a, me],
            device_id={"seq": to},
            device_id_type=pl.DeviceIdType.MESH,
        )

    def returned(a, frm):
        src, dst = outs[a]
        return pltpu.make_async_remote_copy(
            src_ref=src.at[frm],
            dst_ref=dst.at[:, columns(frm)],
            send_sem=out_send.at[a, frm],
            recv_sem=out_recv.at[a, frm],
            device_id={"seq": frm},
            device_id_type=pl.DeviceIdType.MESH,
        )

    def keep(a):
        src, dst = outs[a]
        return pltpu.make_async_copy(src.at[me], dst.at[:, columns(me)], out_local.at[a])

    def over(body):
        def step(i, carry):
            body(i)
            return carry

        lax.fori_loop(1, n, step, 0)

    barrier = pltpu.get_barrier_semaphore()

    @over
    def _(i):
        to = lax.rem(me + i, n)
        pl.semaphore_signal(
            barrier, inc=1, device_id={"seq": to}, device_id_type=pl.DeviceIdType.MESH
        )

    for a in range(4):
        stay(a).start()
    pl.semaphore_wait(barrier, n - 1)

    @over
    def _(i):
        to = lax.rem(me + i, n)
        scatter(0, to).start()
        scatter(1, to).start()

    @over
    def _(i):
        to = lax.rem(me + i, n)
        scatter(2, to).start()
        scatter(3, to).start()

    def note(i, carry):
        block = lax.rem(me + n - i, n)
        part[i] = matching[assign[me, block]]
        return carry

    lax.fori_loop(0, n, note, 0)
    sum_k[...] = jnp.zeros_like(sum_k)
    sum_v[...] = jnp.zeros_like(sum_v)
    for a in range(4):
        stay(a).wait()

    @over
    def _(i):
        frm = lax.rem(me + n - i, n)
        arrival(0, frm).wait_recv()
        arrival(1, frm).wait_recv()

    def work(i):
        block = lax.rem(me + n - i, n)
        chosen = part[i]
        before = jnp.int32(n)
        for j in range(n):
            before = jnp.where((part[j] == chosen) & (j < i), jnp.int32(j), before)
        query, cot = q_all[block], c_all[block]
        key_own, key_far = k_all[block], k_all[chosen]
        value_own, value_far = v_all[block], v_all[chosen]
        s_own = nt(query, key_own) * power
        s_far = nt(query, key_far) * power
        dp_own = nt(cot, value_own)
        dp_far = nt(cot, value_far)
        highest = jnp.maximum(
            jnp.max(s_own, axis=-1, keepdims=True), jnp.max(s_far, axis=-1, keepdims=True)
        )
        e_own = jnp.exp2(s_own - highest)
        e_far = jnp.exp2(s_far - highest)
        total = jnp.sum(e_own, axis=-1, keepdims=True) + jnp.sum(e_far, axis=-1, keepdims=True)
        scale = 1.0 / total
        p_own, p_far = e_own * scale, e_far * scale
        low_own, low_far = p_own.astype(jnp.bfloat16), p_far.astype(jnp.bfloat16)
        attended = (nn(low_own, value_own) + nn(low_far, value_far)).astype(jnp.bfloat16)
        att_out[block] = attended
        row_dot = jnp.sum(
            cot.astype(jnp.float32) * attended.astype(jnp.float32), axis=-1, keepdims=True
        )
        ds_own = (p_own * (dp_own - row_dot) * factor).astype(jnp.bfloat16)
        ds_far = (p_far * (dp_far - row_dot) * factor).astype(jnp.bfloat16)
        gq_out[block] = (nn(ds_own, key_own) + nn(ds_far, key_far)).astype(jnp.bfloat16)
        own_k[block] = tn(ds_own, query)
        own_v[block] = tn(low_own, cot)
        far_k = tn(ds_far, query).astype(jnp.bfloat16).astype(jnp.float32)
        far_v = tn(low_far, cot).astype(jnp.bfloat16).astype(jnp.float32)
        sum_k[i] = sum_k[before] + far_k
        sum_v[i] = sum_v[before] + far_v

    work(0)
    keep(0).start()
    keep(1).start()

    @over
    def _(i):
        block = lax.rem(me + n - i, n)
        arrival(2, block).wait_recv()
        arrival(3, block).wait_recv()
        work(i)
        give(0, block).start()
        give(1, block).start()

    def finish(target):
        last = jnp.int32(n)
        for j in range(n):
            last = jnp.where(part[j] == target, jnp.int32(j), last)
        recv_k = sum_k[last].astype(jnp.bfloat16).astype(jnp.float32)
        recv_v = sum_v[last].astype(jnp.bfloat16).astype(jnp.float32)
        gk_out[target] = (own_k[target] + recv_k).astype(jnp.bfloat16)
        gv_out[target] = (own_v[target] + recv_v).astype(jnp.bfloat16)

    @over
    def _(i):
        target = lax.rem(me + i, n)
        finish(target)
        give(2, target).start()
        give(3, target).start()

    finish(me)
    keep(2).start()
    keep(3).start()

    @over
    def _(i):
        other = lax.rem(me + n - i, n)
        for a in range(4):
            arrival(a, other).wait_send()
            returned(a, other).wait_send()
            returned(a, other).wait_recv()

    for a in range(4):
        keep(a).wait()


def by_heads(queries, keys_in, values_in, cotangent, matching, assign):
    n = lax.axis_size("seq")
    rows, width = queries.shape
    panels = (n, rows, HEAD_DIM)
    anywhere = pl.BlockSpec(memory_space=pl.ANY)
    scalars = pl.BlockSpec(memory_space=pltpu.SMEM)
    flops = 12 * 2 * n * rows * rows * HEAD_DIM
    return pl.pallas_call(
        functools.partial(head_kernel, n),
        out_shape=[jax.ShapeDtypeStruct((rows, width), jnp.bfloat16)] * 4,
        in_specs=[scalars, scalars] + [anywhere] * 4,
        out_specs=[anywhere] * 4,
        scratch_shapes=[pltpu.VMEM(panels, jnp.bfloat16)] * 8
        + [pltpu.VMEM(panels, jnp.float32)] * 2
        + [pltpu.VMEM((n + 1, rows, HEAD_DIM), jnp.float32)] * 2
        + [
            pltpu.SMEM((n,), jnp.int32),
            pltpu.SemaphoreType.DMA((4, n)),
            pltpu.SemaphoreType.DMA((4, n)),
            pltpu.SemaphoreType.DMA((4,)),
            pltpu.SemaphoreType.DMA((4, n)),
            pltpu.SemaphoreType.DMA((4, n)),
            pltpu.SemaphoreType.DMA((4,)),
        ],
        compiler_params=pltpu.CompilerParams(
            collective_id=0, has_side_effects=True, vmem_limit_bytes=48 * 1024 * 1024
        ),
        cost_estimate=pl.CostEstimate(
            flops=flops, bytes_accessed=16 * rows * width, transcendentals=2 * n * rows * rows
        ),
    )(matching, assign, queries, keys_in, values_in, cotangent)


def per_device(queries, keys_in, values_in, cotangent, matching, assign):
    n = lax.axis_size("seq")
    if n == HEADS and queries.shape == (BLOCK, HEADS * HEAD_DIM):
        return tuple(by_heads(queries, keys_in, values_in, cotangent, matching, assign))
    return by_columns(queries, keys_in, values_in, cotangent, matching, assign)


def solution(mesh):
    in_specs = (
        P(("groups", "seq"), None),
        P(("groups", "seq"), None),
        P(("groups", "seq"), None),
        P(("groups", "seq"), None),
        P("groups"),
        P("groups", None),
    )
    out_specs = (
        P(("groups", "seq"), None),
        P(("groups", "seq"), None),
        P(("groups", "seq"), None),
        P(("groups", "seq"), None),
    )
    return jax.shard_map(
        per_device, mesh=mesh, in_specs=in_specs, out_specs=out_specs, check_vma=False
    )
```

```python
import functools

import jax
import jax.numpy as jnp
from jax import lax
from jax.experimental import pallas as pl
from jax.experimental.pallas import tpu as pltpu
from jax.sharding import PartitionSpec as P

BLOCK = 256
HEADS = 16
HEAD_DIM = 128


def to_columns(panel, seq_size, slice_width):
    blocks_dev = panel.shape[0] // BLOCK
    shaped = panel.reshape(blocks_dev, BLOCK, seq_size, slice_width).transpose(2, 0, 1, 3)
    return shaped.reshape(seq_size, blocks_dev, BLOCK * slice_width)


def from_columns(moved, seq_size, slice_width):
    blocks_dev = moved.shape[1]
    shaped = moved.reshape(seq_size, blocks_dev, BLOCK, slice_width).transpose(1, 2, 0, 3)
    return shaped.reshape(blocks_dev * BLOCK, seq_size * slice_width)


def by_columns(queries, keys_in, values_in, cotangent, matching, assign):
    seq_size = lax.axis_size("seq")
    tok_dev, feature_count = queries.shape
    blocks_dev = tok_dev // BLOCK
    total_blocks = matching.shape[0]
    partner = jnp.take(matching, assign, axis=0)
    targets = jnp.arange(total_blocks, dtype=jnp.int32)
    slice_width = feature_count // seq_size
    factor = HEAD_DIM ** (-0.5)

    def column_row():
        head_here = lax.axis_index("seq") * slice_width // HEAD_DIM
        return lax.dynamic_index_in_dim(partner, head_here, 0, keepdims=False)

    shape4 = (blocks_dev, BLOCK, HEADS, HEAD_DIM)
    query_blocks = queries.reshape(shape4)
    cot_blocks = cotangent.reshape(shape4)
    row_here = column_row()
    select_here = (targets[None, :] == row_here[:, None]).astype(jnp.bfloat16)

    def pick_one(piece):
        moved = jnp.dot(
            select_here, piece.reshape(total_blocks, -1), preferred_element_type=jnp.float32
        )
        return moved.astype(jnp.bfloat16).reshape(piece.shape)

    pieces = (
        lax.all_to_all(
            to_columns(keys_in, seq_size, slice_width),
            "seq",
            split_axis=0,
            concat_axis=0,
            tiled=True,
        ),
        lax.all_to_all(
            to_columns(values_in, seq_size, slice_width),
            "seq",
            split_axis=0,
            concat_axis=0,
            tiled=True,
        ),
    )
    got_first = lax.all_to_all(pick_one(pieces[0]), "seq", split_axis=0, concat_axis=0, tiled=True)
    got_second = lax.all_to_all(pick_one(pieces[1]), "seq", split_axis=0, concat_axis=0, tiled=True)
    key_far = from_columns(got_first, seq_size, slice_width)
    value_far = from_columns(got_second, seq_size, slice_width)
    key_cat = jnp.concatenate([keys_in.reshape(shape4), key_far.reshape(shape4)], axis=1)
    value_cat = jnp.concatenate([values_in.reshape(shape4), value_far.reshape(shape4)], axis=1)
    scores = (
        jnp.einsum("bqhd,bkhd->bhqk", query_blocks, key_cat, preferred_element_type=jnp.float32)
        * factor
    )
    highest = jnp.max(scores, axis=-1, keepdims=True)
    raised = jnp.exp(scores - highest)
    weights = raised / jnp.sum(raised, axis=-1, keepdims=True)
    key_cat, value_cat, weights, weights_low = (
        key_cat,
        value_cat,
        weights,
        weights.astype(jnp.bfloat16),
    )
    out_blocks = jnp.einsum(
        "bhqk,bkhd->bqhd", weights_low, value_cat, preferred_element_type=jnp.float32
    ).astype(jnp.bfloat16)
    dprobs = jnp.einsum(
        "bqhd,bkhd->bhqk", cot_blocks, value_cat, preferred_element_type=jnp.float32
    )
    row_dot = jnp.einsum(
        "bqhd,bqhd->bhq", cot_blocks, out_blocks, preferred_element_type=jnp.float32
    )
    dscores = (weights * (dprobs - row_dot[..., None]) * factor).astype(jnp.bfloat16)
    grad_query = jnp.einsum(
        "bhqk,bkhd->bqhd", dscores, key_cat, preferred_element_type=jnp.float32
    ).astype(jnp.bfloat16)
    dkey_cat = jnp.einsum(
        "bhqk,bqhd->bkhd", dscores, query_blocks, preferred_element_type=jnp.float32
    )
    dvalue_cat = jnp.einsum(
        "bhqk,bqhd->bkhd", weights_low, cot_blocks, preferred_element_type=jnp.float32
    )
    far_keys = dkey_cat[:, BLOCK:].astype(jnp.bfloat16).reshape(tok_dev, feature_count)
    far_values = dvalue_cat[:, BLOCK:].astype(jnp.bfloat16).reshape(tok_dev, feature_count)
    row_here = column_row()
    onehot_here = (row_here[None, :] == targets[:, None]).astype(jnp.bfloat16)

    def add_columns(piece):
        summed = jnp.dot(
            onehot_here, piece.reshape(total_blocks, -1), preferred_element_type=jnp.float32
        )
        return summed.astype(jnp.bfloat16).reshape(piece.shape)

    pieces = (
        lax.all_to_all(
            to_columns(far_keys, seq_size, slice_width),
            "seq",
            split_axis=0,
            concat_axis=0,
            tiled=True,
        ),
        lax.all_to_all(
            to_columns(far_values, seq_size, slice_width),
            "seq",
            split_axis=0,
            concat_axis=0,
            tiled=True,
        ),
    )
    got_first = lax.all_to_all(
        add_columns(pieces[0]), "seq", split_axis=0, concat_axis=0, tiled=True
    )
    got_second = lax.all_to_all(
        add_columns(pieces[1]), "seq", split_axis=0, concat_axis=0, tiled=True
    )
    recv_keys = from_columns(got_first, seq_size, slice_width)
    recv_values = from_columns(got_second, seq_size, slice_width)
    grad_keys = (
        dkey_cat[:, :BLOCK].reshape(tok_dev, feature_count) + recv_keys.astype(jnp.float32)
    ).astype(jnp.bfloat16)
    grad_values = (
        dvalue_cat[:, :BLOCK].reshape(tok_dev, feature_count) + recv_values.astype(jnp.float32)
    ).astype(jnp.bfloat16)
    return (
        out_blocks.reshape(tok_dev, feature_count),
        grad_query.reshape(tok_dev, feature_count),
        grad_keys,
        grad_values,
    )


def nt(a, b):
    return lax.dot_general(a, b, (((1,), (1,)), ((), ())), preferred_element_type=jnp.float32)


def tn(a, b):
    return lax.dot_general(a, b, (((0,), (0,)), ((), ())), preferred_element_type=jnp.float32)


def nn(a, b):
    return lax.dot_general(a, b, (((1,), (0,)), ((), ())), preferred_element_type=jnp.float32)


def head_kernel(
    n,
    matching_ref,
    assign_ref,
    q_ref,
    k_ref,
    v_ref,
    c_ref,
    att_ref,
    gq_ref,
    gk_ref,
    gv_ref,
    q_all,
    k_all,
    v_all,
    c_all,
    att_out,
    gq_out,
    gk_out,
    gv_out,
    own_k,
    own_v,
    sum_k,
    sum_v,
    matching,
    assign,
    part,
    scalar_sem,
    in_send,
    in_recv,
    in_local,
    out_send,
    out_recv,
    out_local,
):
    me = lax.axis_index("seq")
    factor = HEAD_DIM ** (-0.5)
    power = factor * 1.4426950408889634
    ins = ((k_ref, k_all), (v_ref, v_all), (q_ref, q_all), (c_ref, c_all))
    outs = ((att_out, att_ref), (gq_out, gq_ref), (gk_out, gk_ref), (gv_out, gv_ref))

    def columns(index):
        return pl.ds(pl.multiple_of(index * HEAD_DIM, HEAD_DIM), HEAD_DIM)

    def scatter(a, to):
        src, dst = ins[a]
        return pltpu.make_async_remote_copy(
            src_ref=src.at[:, columns(to)],
            dst_ref=dst.at[me],
            send_sem=in_send.at[a, to],
            recv_sem=in_recv.at[a, me],
            device_id={"seq": to},
            device_id_type=pl.DeviceIdType.MESH,
        )

    def arrival(a, frm):
        src, dst = ins[a]
        return pltpu.make_async_remote_copy(
            src_ref=src.at[:, columns(frm)],
            dst_ref=dst.at[frm],
            send_sem=in_send.at[a, frm],
            recv_sem=in_recv.at[a, frm],
            device_id={"seq": frm},
            device_id_type=pl.DeviceIdType.MESH,
        )

    def stay(a):
        src, dst = ins[a]
        return pltpu.make_async_copy(src.at[:, columns(me)], dst.at[me], in_local.at[a])

    def give(a, to):
        src, dst = outs[a]
        return pltpu.make_async_remote_copy(
            src_ref=src.at[to],
            dst_ref=dst.at[:, columns(me)],
            send_sem=out_send.at[a, to],
            recv_sem=out_recv.at[a, me],
            device_id={"seq": to},
            device_id_type=pl.DeviceIdType.MESH,
        )

    def returned(a, frm):
        src, dst = outs[a]
        return pltpu.make_async_remote_copy(
            src_ref=src.at[frm],
            dst_ref=dst.at[:, columns(frm)],
            send_sem=out_send.at[a, frm],
            recv_sem=out_recv.at[a, frm],
            device_id={"seq": frm},
            device_id_type=pl.DeviceIdType.MESH,
        )

    def keep(a):
        src, dst = outs[a]
        return pltpu.make_async_copy(src.at[me], dst.at[:, columns(me)], out_local.at[a])

    half = n // 2
    here = me // half
    place = lax.rem(me, half)

    def ahead(i):
        side = lax.rem(here + i // half, 2)
        return side * half + lax.rem(place + i, half)

    def behind(i):
        side = lax.rem(here + i // half, 2)
        return side * half + lax.rem(place + n - i, half)

    def over(start, stop):
        def run(body):
            def step(i, carry):
                body(i)
                return carry

            lax.fori_loop(start, stop, step, 0)

        return run

    barrier = pltpu.get_barrier_semaphore()

    scalars = (
        pltpu.make_async_copy(matching_ref, matching, scalar_sem.at[0]),
        pltpu.make_async_copy(assign_ref, assign, scalar_sem.at[1]),
    )
    for copy in scalars:
        copy.start()

    @over(1, n)
    def _(i):
        to = ahead(i)
        pl.semaphore_signal(
            barrier, inc=1, device_id={"seq": to}, device_id_type=pl.DeviceIdType.MESH
        )

    for a in range(4):
        stay(a).start()
    pl.semaphore_wait(barrier, n - 1)

    for start, stop, pair in ((half, n, (0, 1)), (half, n, (2, 3)), (1, half, (0, 1)), (1, half, (2, 3))):

        @over(start, stop)
        def _(i):
            to = ahead(i)
            scatter(pair[0], to).start()
            scatter(pair[1], to).start()

    for copy in scalars:
        copy.wait()

    def note(i, carry):
        block = behind(i)
        part[i] = matching[assign[me, block]]
        return carry

    lax.fori_loop(0, n, note, 0)
    sum_k[...] = jnp.zeros_like(sum_k)
    sum_v[...] = jnp.zeros_like(sum_v)
    for a in range(4):
        stay(a).wait()

    @over(1, n)
    def _(i):
        frm = behind(i)
        arrival(0, frm).wait_recv()
        arrival(1, frm).wait_recv()

    def work(i):
        block = behind(i)
        chosen = part[i]
        before = jnp.int32(n)
        for j in range(n):
            before = jnp.where((part[j] == chosen) & (j < i), jnp.int32(j), before)
        query, cot = q_all[block], c_all[block]
        key_own, key_far = k_all[block], k_all[chosen]
        value_own, value_far = v_all[block], v_all[chosen]
        s_own = nt(query, key_own) * power
        s_far = nt(query, key_far) * power
        dp_own = nt(cot, value_own)
        dp_far = nt(cot, value_far)
        highest = jnp.maximum(
            jnp.max(s_own, axis=-1, keepdims=True), jnp.max(s_far, axis=-1, keepdims=True)
        )
        e_own = jnp.exp2(s_own - highest)
        e_far = jnp.exp2(s_far - highest)
        total = jnp.sum(e_own, axis=-1, keepdims=True) + jnp.sum(e_far, axis=-1, keepdims=True)
        scale = 1.0 / total
        p_own, p_far = e_own * scale, e_far * scale
        low_own, low_far = p_own.astype(jnp.bfloat16), p_far.astype(jnp.bfloat16)
        attended = (nn(low_own, value_own) + nn(low_far, value_far)).astype(jnp.bfloat16)
        att_out[block] = attended
        row_dot = jnp.sum(
            cot.astype(jnp.float32) * attended.astype(jnp.float32), axis=-1, keepdims=True
        )
        ds_own = (p_own * (dp_own - row_dot) * factor).astype(jnp.bfloat16)
        ds_far = (p_far * (dp_far - row_dot) * factor).astype(jnp.bfloat16)
        gq_out[block] = (nn(ds_own, key_own) + nn(ds_far, key_far)).astype(jnp.bfloat16)
        own_k[block] = tn(ds_own, query)
        own_v[block] = tn(low_own, cot)
        far_k = tn(ds_far, query).astype(jnp.bfloat16).astype(jnp.float32)
        far_v = tn(low_far, cot).astype(jnp.bfloat16).astype(jnp.float32)
        sum_k[i] = sum_k[before] + far_k
        sum_v[i] = sum_v[before] + far_v

    work(0)
    keep(0).start()
    keep(1).start()

    @over(1, n)
    def _(i):
        block = behind(i)
        arrival(2, block).wait_recv()
        arrival(3, block).wait_recv()
        work(i)
        give(0, block).start()
        give(1, block).start()

    def finish(target):
        last = jnp.int32(n)
        for j in range(n):
            last = jnp.where(part[j] == target, jnp.int32(j), last)
        recv_k = sum_k[last].astype(jnp.bfloat16).astype(jnp.float32)
        recv_v = sum_v[last].astype(jnp.bfloat16).astype(jnp.float32)
        gk_out[target] = (own_k[target] + recv_k).astype(jnp.bfloat16)
        gv_out[target] = (own_v[target] + recv_v).astype(jnp.bfloat16)

    for start, stop in ((half, n), (1, half)):

        @over(start, stop)
        def _(i):
            target = ahead(i)
            finish(target)
            give(2, target).start()
            give(3, target).start()

    finish(me)
    keep(2).start()
    keep(3).start()

    @over(1, n)
    def _(i):
        other = behind(i)
        for a in range(4):
            arrival(a, other).wait_send()
            returned(a, other).wait_send()
            returned(a, other).wait_recv()

    for a in range(4):
        keep(a).wait()


def hand_over(*refs):
    copies = [pltpu.make_async_copy(refs[a], refs[4 + a], refs[8].at[a]) for a in range(4)]
    for copy in copies:
        copy.start()
    for copy in copies:
        copy.wait()


def by_heads(queries, keys_in, values_in, cotangent, matching, assign):
    n = lax.axis_size("seq")
    rows, width = queries.shape
    panels = (n, rows, HEAD_DIM)
    anywhere = pl.BlockSpec(memory_space=pl.ANY)
    flops = 12 * 2 * n * rows * rows * HEAD_DIM
    results = pl.pallas_call(
        functools.partial(head_kernel, n),
        out_shape=[jax.ShapeDtypeStruct((rows, width), jnp.bfloat16)] * 4,
        in_specs=[anywhere] * 6,
        out_specs=[anywhere] * 4,
        scratch_shapes=[pltpu.VMEM(panels, jnp.bfloat16)] * 8
        + [pltpu.VMEM(panels, jnp.float32)] * 2
        + [pltpu.VMEM((n + 1, rows, HEAD_DIM), jnp.float32)] * 2
        + [
            pltpu.SMEM(matching.shape, jnp.int32),
            pltpu.SMEM(assign.shape, jnp.int32),
            pltpu.SMEM((n,), jnp.int32),
            pltpu.SemaphoreType.DMA((2,)),
            pltpu.SemaphoreType.DMA((4, n)),
            pltpu.SemaphoreType.DMA((4, n)),
            pltpu.SemaphoreType.DMA((4,)),
            pltpu.SemaphoreType.DMA((4, n)),
            pltpu.SemaphoreType.DMA((4, n)),
            pltpu.SemaphoreType.DMA((4,)),
        ],
        compiler_params=pltpu.CompilerParams(
            collective_id=0, has_side_effects=True, vmem_limit_bytes=48 * 1024 * 1024
        ),
        cost_estimate=pl.CostEstimate(
            flops=flops, bytes_accessed=16 * rows * width, transcendentals=2 * n * rows * rows
        ),
    )(matching, assign, queries, keys_in, values_in, cotangent)
    return pl.pallas_call(
        hand_over,
        out_shape=[jax.ShapeDtypeStruct((rows, width), jnp.bfloat16)] * 4,
        in_specs=[pl.BlockSpec(memory_space=pltpu.VMEM)] * 4,
        out_specs=[anywhere] * 4,
        scratch_shapes=[pltpu.SemaphoreType.DMA((4,))],
        compiler_params=pltpu.CompilerParams(vmem_limit_bytes=16 * 1024 * 1024),
    )(*results)


def per_device(queries, keys_in, values_in, cotangent, matching, assign):
    n = lax.axis_size("seq")
    if n == HEADS and queries.shape == (BLOCK, HEADS * HEAD_DIM):
        return tuple(by_heads(queries, keys_in, values_in, cotangent, matching, assign))
    return by_columns(queries, keys_in, values_in, cotangent, matching, assign)


def solution(mesh):
    in_specs = (
        P(("groups", "seq"), None),
        P(("groups", "seq"), None),
        P(("groups", "seq"), None),
        P(("groups", "seq"), None),
        P("groups"),
        P("groups", None),
    )
    out_specs = (
        P(("groups", "seq"), None),
        P(("groups", "seq"), None),
        P(("groups", "seq"), None),
        P(("groups", "seq"), None),
    )
    return jax.shard_map(
        per_device, mesh=mesh, in_specs=in_specs, out_specs=out_specs, check_vma=False
    )
```

```python
import functools

import jax
import jax.numpy as jnp
from jax import lax
from jax.experimental import pallas as pl
from jax.experimental.pallas import tpu as pltpu
from jax.sharding import PartitionSpec as P

BLOCK = 256
HEADS = 16
HEAD_DIM = 128


def to_columns(panel, seq_size, slice_width):
    blocks_dev = panel.shape[0] // BLOCK
    shaped = panel.reshape(blocks_dev, BLOCK, seq_size, slice_width).transpose(2, 0, 1, 3)
    return shaped.reshape(seq_size, blocks_dev, BLOCK * slice_width)


def from_columns(moved, seq_size, slice_width):
    blocks_dev = moved.shape[1]
    shaped = moved.reshape(seq_size, blocks_dev, BLOCK, slice_width).transpose(1, 2, 0, 3)
    return shaped.reshape(blocks_dev * BLOCK, seq_size * slice_width)


def by_columns(queries, keys_in, values_in, cotangent, matching, assign):
    seq_size = lax.axis_size("seq")
    tok_dev, feature_count = queries.shape
    blocks_dev = tok_dev // BLOCK
    total_blocks = matching.shape[0]
    partner = jnp.take(matching, assign, axis=0)
    targets = jnp.arange(total_blocks, dtype=jnp.int32)
    slice_width = feature_count // seq_size
    factor = HEAD_DIM ** (-0.5)

    def column_row():
        head_here = lax.axis_index("seq") * slice_width // HEAD_DIM
        return lax.dynamic_index_in_dim(partner, head_here, 0, keepdims=False)

    shape4 = (blocks_dev, BLOCK, HEADS, HEAD_DIM)
    query_blocks = queries.reshape(shape4)
    cot_blocks = cotangent.reshape(shape4)
    row_here = column_row()
    select_here = (targets[None, :] == row_here[:, None]).astype(jnp.bfloat16)

    def pick_one(piece):
        moved = jnp.dot(
            select_here, piece.reshape(total_blocks, -1), preferred_element_type=jnp.float32
        )
        return moved.astype(jnp.bfloat16).reshape(piece.shape)

    pieces = (
        lax.all_to_all(
            to_columns(keys_in, seq_size, slice_width),
            "seq",
            split_axis=0,
            concat_axis=0,
            tiled=True,
        ),
        lax.all_to_all(
            to_columns(values_in, seq_size, slice_width),
            "seq",
            split_axis=0,
            concat_axis=0,
            tiled=True,
        ),
    )
    got_first = lax.all_to_all(pick_one(pieces[0]), "seq", split_axis=0, concat_axis=0, tiled=True)
    got_second = lax.all_to_all(pick_one(pieces[1]), "seq", split_axis=0, concat_axis=0, tiled=True)
    key_far = from_columns(got_first, seq_size, slice_width)
    value_far = from_columns(got_second, seq_size, slice_width)
    key_cat = jnp.concatenate([keys_in.reshape(shape4), key_far.reshape(shape4)], axis=1)
    value_cat = jnp.concatenate([values_in.reshape(shape4), value_far.reshape(shape4)], axis=1)
    scores = (
        jnp.einsum("bqhd,bkhd->bhqk", query_blocks, key_cat, preferred_element_type=jnp.float32)
        * factor
    )
    highest = jnp.max(scores, axis=-1, keepdims=True)
    raised = jnp.exp(scores - highest)
    weights = raised / jnp.sum(raised, axis=-1, keepdims=True)
    key_cat, value_cat, weights, weights_low = (
        key_cat,
        value_cat,
        weights,
        weights.astype(jnp.bfloat16),
    )
    out_blocks = jnp.einsum(
        "bhqk,bkhd->bqhd", weights_low, value_cat, preferred_element_type=jnp.float32
    ).astype(jnp.bfloat16)
    dprobs = jnp.einsum(
        "bqhd,bkhd->bhqk", cot_blocks, value_cat, preferred_element_type=jnp.float32
    )
    row_dot = jnp.einsum(
        "bqhd,bqhd->bhq", cot_blocks, out_blocks, preferred_element_type=jnp.float32
    )
    dscores = (weights * (dprobs - row_dot[..., None]) * factor).astype(jnp.bfloat16)
    grad_query = jnp.einsum(
        "bhqk,bkhd->bqhd", dscores, key_cat, preferred_element_type=jnp.float32
    ).astype(jnp.bfloat16)
    dkey_cat = jnp.einsum(
        "bhqk,bqhd->bkhd", dscores, query_blocks, preferred_element_type=jnp.float32
    )
    dvalue_cat = jnp.einsum(
        "bhqk,bqhd->bkhd", weights_low, cot_blocks, preferred_element_type=jnp.float32
    )
    far_keys = dkey_cat[:, BLOCK:].astype(jnp.bfloat16).reshape(tok_dev, feature_count)
    far_values = dvalue_cat[:, BLOCK:].astype(jnp.bfloat16).reshape(tok_dev, feature_count)
    row_here = column_row()
    onehot_here = (row_here[None, :] == targets[:, None]).astype(jnp.bfloat16)

    def add_columns(piece):
        summed = jnp.dot(
            onehot_here, piece.reshape(total_blocks, -1), preferred_element_type=jnp.float32
        )
        return summed.astype(jnp.bfloat16).reshape(piece.shape)

    pieces = (
        lax.all_to_all(
            to_columns(far_keys, seq_size, slice_width),
            "seq",
            split_axis=0,
            concat_axis=0,
            tiled=True,
        ),
        lax.all_to_all(
            to_columns(far_values, seq_size, slice_width),
            "seq",
            split_axis=0,
            concat_axis=0,
            tiled=True,
        ),
    )
    got_first = lax.all_to_all(
        add_columns(pieces[0]), "seq", split_axis=0, concat_axis=0, tiled=True
    )
    got_second = lax.all_to_all(
        add_columns(pieces[1]), "seq", split_axis=0, concat_axis=0, tiled=True
    )
    recv_keys = from_columns(got_first, seq_size, slice_width)
    recv_values = from_columns(got_second, seq_size, slice_width)
    grad_keys = (
        dkey_cat[:, :BLOCK].reshape(tok_dev, feature_count) + recv_keys.astype(jnp.float32)
    ).astype(jnp.bfloat16)
    grad_values = (
        dvalue_cat[:, :BLOCK].reshape(tok_dev, feature_count) + recv_values.astype(jnp.float32)
    ).astype(jnp.bfloat16)
    return (
        out_blocks.reshape(tok_dev, feature_count),
        grad_query.reshape(tok_dev, feature_count),
        grad_keys,
        grad_values,
    )


def nt(a, b):
    return lax.dot_general(a, b, (((1,), (1,)), ((), ())), preferred_element_type=jnp.float32)


def tn(a, b):
    return lax.dot_general(a, b, (((0,), (0,)), ((), ())), preferred_element_type=jnp.float32)


def nn(a, b):
    return lax.dot_general(a, b, (((1,), (0,)), ((), ())), preferred_element_type=jnp.float32)


def head_kernel(
    n,
    matching_ref,
    assign_ref,
    q_ref,
    k_ref,
    v_ref,
    c_ref,
    att_ref,
    gq_ref,
    gk_ref,
    gv_ref,
    q_all,
    k_all,
    v_all,
    c_all,
    att_out,
    gq_out,
    gk_out,
    gv_out,
    own_k,
    own_v,
    sum_k,
    sum_v,
    matching,
    assign,
    part,
    scalar_sem,
    in_send,
    in_recv,
    in_local,
    out_send,
    out_recv,
    out_local,
):
    me = lax.axis_index("seq")
    factor = HEAD_DIM ** (-0.5)
    power = factor * 1.4426950408889634
    ins = ((k_ref, k_all), (v_ref, v_all), (q_ref, q_all), (c_ref, c_all))
    outs = ((att_out, att_ref), (gq_out, gq_ref), (gk_out, gk_ref), (gv_out, gv_ref))

    def columns(index):
        return pl.ds(pl.multiple_of(index * HEAD_DIM, HEAD_DIM), HEAD_DIM)

    def scatter(a, to):
        src, dst = ins[a]
        return pltpu.make_async_remote_copy(
            src_ref=src.at[:, columns(to)],
            dst_ref=dst.at[me],
            send_sem=in_send.at[a, to],
            recv_sem=in_recv.at[a, me],
            device_id={"seq": to},
            device_id_type=pl.DeviceIdType.MESH,
        )

    def arrival(a, frm):
        src, dst = ins[a]
        return pltpu.make_async_remote_copy(
            src_ref=src.at[:, columns(frm)],
            dst_ref=dst.at[frm],
            send_sem=in_send.at[a, frm],
            recv_sem=in_recv.at[a, frm],
            device_id={"seq": frm},
            device_id_type=pl.DeviceIdType.MESH,
        )

    def stay(a):
        src, dst = ins[a]
        return pltpu.make_async_copy(src.at[:, columns(me)], dst.at[me], in_local.at[a])

    def give(a, to):
        src, dst = outs[a]
        return pltpu.make_async_remote_copy(
            src_ref=src.at[to],
            dst_ref=dst.at[:, columns(me)],
            send_sem=out_send.at[a, to],
            recv_sem=out_recv.at[a, me],
            device_id={"seq": to},
            device_id_type=pl.DeviceIdType.MESH,
        )

    def returned(a, frm):
        src, dst = outs[a]
        return pltpu.make_async_remote_copy(
            src_ref=src.at[frm],
            dst_ref=dst.at[:, columns(frm)],
            send_sem=out_send.at[a, frm],
            recv_sem=out_recv.at[a, frm],
            device_id={"seq": frm},
            device_id_type=pl.DeviceIdType.MESH,
        )

    def keep(a):
        src, dst = outs[a]
        return pltpu.make_async_copy(src.at[me], dst.at[:, columns(me)], out_local.at[a])

    half = n // 2
    here = me // half
    place = lax.rem(me, half)

    def ahead(i):
        side = lax.rem(here + i // half, 2)
        return side * half + lax.rem(place + i, half)

    def behind(i):
        side = lax.rem(here + i // half, 2)
        return side * half + lax.rem(place + n - i, half)

    def over(start, stop):
        def run(body):
            def step(i, carry):
                body(i)
                return carry

            lax.fori_loop(start, stop, step, 0)

        return run

    barrier = pltpu.get_barrier_semaphore()

    scalars = (
        pltpu.make_async_copy(matching_ref, matching, scalar_sem.at[0]),
        pltpu.make_async_copy(assign_ref, assign, scalar_sem.at[1]),
    )
    for copy in scalars:
        copy.start()

    @over(1, n)
    def _(i):
        to = ahead(i)
        pl.semaphore_signal(
            barrier, inc=1, device_id={"seq": to}, device_id_type=pl.DeviceIdType.MESH
        )

    for a in range(4):
        stay(a).start()
    pl.semaphore_wait(barrier, n - 1)

    for start, stop, pair in ((half, n, (0, 1)), (half, n, (2, 3)), (1, half, (0, 1)), (1, half, (2, 3))):

        @over(start, stop)
        def _(i):
            to = ahead(i)
            scatter(pair[0], to).start()
            scatter(pair[1], to).start()

    for copy in scalars:
        copy.wait()

    def note(i, carry):
        block = behind(i)
        part[i] = matching[assign[me, block]]
        return carry

    lax.fori_loop(0, n, note, 0)
    sum_k[...] = jnp.zeros_like(sum_k)
    sum_v[...] = jnp.zeros_like(sum_v)
    for a in range(4):
        stay(a).wait()

    @over(1, n)
    def _(i):
        frm = behind(i)
        arrival(0, frm).wait_recv()
        arrival(1, frm).wait_recv()

    def work(i):
        block = behind(i)
        chosen = part[i]
        before = jnp.int32(n)
        for j in range(n):
            before = jnp.where((part[j] == chosen) & (j < i), jnp.int32(j), before)
        query, cot = q_all[block], c_all[block]
        key_own, key_far = k_all[block], k_all[chosen]
        value_own, value_far = v_all[block], v_all[chosen]
        s_own = nt(query, key_own) * power
        s_far = nt(query, key_far) * power
        dp_own = nt(cot, value_own)
        dp_far = nt(cot, value_far)
        highest = jnp.maximum(
            jnp.max(s_own, axis=-1, keepdims=True), jnp.max(s_far, axis=-1, keepdims=True)
        )
        e_own = jnp.exp2(s_own - highest)
        e_far = jnp.exp2(s_far - highest)
        total = jnp.sum(e_own, axis=-1, keepdims=True) + jnp.sum(e_far, axis=-1, keepdims=True)
        scale = 1.0 / total
        p_own, p_far = e_own * scale, e_far * scale
        low_own, low_far = p_own.astype(jnp.bfloat16), p_far.astype(jnp.bfloat16)
        attended = (nn(low_own, value_own) + nn(low_far, value_far)).astype(jnp.bfloat16)
        att_out[block] = attended
        row_dot = jnp.sum(
            cot.astype(jnp.float32) * attended.astype(jnp.float32), axis=-1, keepdims=True
        )
        ds_own = (p_own * (dp_own - row_dot) * factor).astype(jnp.bfloat16)
        ds_far = (p_far * (dp_far - row_dot) * factor).astype(jnp.bfloat16)
        gq_out[block] = (nn(ds_own, key_own) + nn(ds_far, key_far)).astype(jnp.bfloat16)
        own_k[block] = tn(ds_own, query)
        own_v[block] = tn(low_own, cot)
        far_k = tn(ds_far, query).astype(jnp.bfloat16).astype(jnp.float32)
        far_v = tn(low_far, cot).astype(jnp.bfloat16).astype(jnp.float32)
        sum_k[i] = sum_k[before] + far_k
        sum_v[i] = sum_v[before] + far_v

    work(0)
    keep(0).start()
    keep(1).start()

    @over(1, n)
    def _(i):
        block = behind(i)
        arrival(2, block).wait_recv()
        arrival(3, block).wait_recv()
        work(i)
        give(0, block).start()
        give(1, block).start()

    def finish(target):
        last = jnp.int32(n)
        for j in range(n):
            last = jnp.where(part[j] == target, jnp.int32(j), last)
        recv_k = sum_k[last].astype(jnp.bfloat16).astype(jnp.float32)
        recv_v = sum_v[last].astype(jnp.bfloat16).astype(jnp.float32)
        gk_out[target] = (own_k[target] + recv_k).astype(jnp.bfloat16)
        gv_out[target] = (own_v[target] + recv_v).astype(jnp.bfloat16)

    for start, stop in ((half, n), (1, half)):

        @over(start, stop)
        def _(i):
            target = ahead(i)
            finish(target)
            give(2, target).start()
            give(3, target).start()

    finish(me)
    keep(2).start()
    keep(3).start()

    @over(1, n)
    def _(i):
        other = behind(i)
        for a in range(4):
            arrival(a, other).wait_send()
            returned(a, other).wait_send()
            returned(a, other).wait_recv()

    for a in range(4):
        keep(a).wait()


def hand_over(*refs):
    copies = [pltpu.make_async_copy(refs[a], refs[4 + a], refs[8].at[a]) for a in range(4)]
    for copy in copies:
        copy.start()
    for copy in copies:
        copy.wait()


def by_heads(queries, keys_in, values_in, cotangent, matching, assign):
    n = lax.axis_size("seq")
    rows, width = queries.shape
    panels = (n, rows, HEAD_DIM)
    anywhere = pl.BlockSpec(memory_space=pl.ANY)
    flops = 12 * 2 * n * rows * rows * HEAD_DIM
    results = pl.pallas_call(
        functools.partial(head_kernel, n),
        out_shape=[jax.ShapeDtypeStruct((rows, width), jnp.bfloat16)] * 4,
        in_specs=[anywhere] * 6,
        out_specs=[anywhere] * 4,
        scratch_shapes=[pltpu.VMEM(panels, jnp.bfloat16)] * 8
        + [pltpu.VMEM(panels, jnp.float32)] * 2
        + [pltpu.VMEM((n + 1, rows, HEAD_DIM), jnp.float32)] * 2
        + [
            pltpu.SMEM(matching.shape, jnp.int32),
            pltpu.SMEM(assign.shape, jnp.int32),
            pltpu.SMEM((n,), jnp.int32),
            pltpu.SemaphoreType.DMA((2,)),
            pltpu.SemaphoreType.DMA((4, n)),
            pltpu.SemaphoreType.DMA((4, n)),
            pltpu.SemaphoreType.DMA((4,)),
            pltpu.SemaphoreType.DMA((4, n)),
            pltpu.SemaphoreType.DMA((4, n)),
            pltpu.SemaphoreType.DMA((4,)),
        ],
        compiler_params=pltpu.CompilerParams(
            collective_id=0, has_side_effects=True, vmem_limit_bytes=52_000_000
        ),
        cost_estimate=pl.CostEstimate(
            flops=flops, bytes_accessed=16 * rows * width, transcendentals=2 * n * rows * rows
        ),
    )(matching, assign, queries, keys_in, values_in, cotangent)
    return pl.pallas_call(
        hand_over,
        out_shape=[jax.ShapeDtypeStruct((rows, width), jnp.bfloat16)] * 4,
        in_specs=[pl.BlockSpec(memory_space=pltpu.VMEM)] * 4,
        out_specs=[anywhere] * 4,
        scratch_shapes=[pltpu.SemaphoreType.DMA((4,))],
        compiler_params=pltpu.CompilerParams(vmem_limit_bytes=16 * 1024 * 1024),
    )(*results)


def per_device(queries, keys_in, values_in, cotangent, matching, assign):
    n = lax.axis_size("seq")
    if n == HEADS and queries.shape == (BLOCK, HEADS * HEAD_DIM):
        return tuple(by_heads(queries, keys_in, values_in, cotangent, matching, assign))
    return by_columns(queries, keys_in, values_in, cotangent, matching, assign)


def solution(mesh):
    in_specs = (
        P(("groups", "seq"), None),
        P(("groups", "seq"), None),
        P(("groups", "seq"), None),
        P(("groups", "seq"), None),
        P("groups"),
        P("groups", None),
    )
    out_specs = (
        P(("groups", "seq"), None),
        P(("groups", "seq"), None),
        P(("groups", "seq"), None),
        P(("groups", "seq"), None),
    )
    return jax.shard_map(
        per_device, mesh=mesh, in_specs=in_specs, out_specs=out_specs, check_vma=False
    )
```
